512 devices in a mesh: row: 32 (over y, x), col: 16 (over z, core).
Axes of the slice: x: 4, y: 8, z: 8, core: 2. Of those that a mesh axis runs over, the one named last changes fastest.
Arguments:
- momentum: float32 [8192, 26624], P('row', 'col')
- weight: bfloat16 [8192, 26624], P('row', 'col'), may hold values from -6 to 6
- init_seed: int32 [1], replicated, may hold values from 0 to 999999
- step_rate: float32 [1], replicated, may hold values from 0.1 to 1
Outputs:
- momentum_next: float32 [8192, 26624], P('row', 'col')
- weight_next: bfloat16 [8192, 26624], P('row', 'col')
- next_factor: float32 [512, 26624], P('row', 'col')
The draws below stay inside these ranges and needn't reach their ends.
All inputs are finite; a program needn't handle non-finite values.
Results may differ from the reference program's by a relative error of at most 0.001.
Values sent between devices are 32-bit elements; how exact they have to be, the bound alone decides.
A program may use at most 64 MiB of HBM per device.

```python
import math
import jax
import jax.numpy as jnp
from jax import lax

ROWS = 8192
COLS = 26624
RANK = 512


def draw_momentum(key, part):
    key = jax.random.fold_in(key, 7)
    col_key, row_key, base_key = jax.random.split(key, 3)
    col_scale = jnp.exp(jax.random.uniform(col_key, (COLS,), jnp.float32, 0.0, math.log(10.0)))
    row_scale = jnp.exp(jax.random.uniform(row_key, (ROWS,), jnp.float32, 0.0, math.log(3.0)))
    base_values = jax.random.normal(base_key, (ROWS, COLS), jnp.float32)
    return base_values * row_scale[:, None] * col_scale[None, :] * 0.25


def shard_levels(rng, shape, pieces, least, top_value):
    factor_of, own = 1.0, jax.random.fold_in(rng, 6)
    for position, blocks in pieces:
        draws = jnp.exp(jax.random.uniform(jax.random.fold_in(own, position), (blocks,), jnp.float32, least / len(pieces), top_value / len(pieces)))
        factor_of = factor_of * jnp.repeat(draws, shape[position] // blocks).reshape([-1 if axis == position else 1 for axis in range(len(shape))])
    return factor_of


def scatter_about(stream_key, extent, deviation, limit, shards=(), kind=jnp.bfloat16):
    drawn = jax.random.normal(stream_key, extent, jnp.float32) * deviation
    if len(shards) > 0:
        drawn = shard_levels(stream_key, extent, shards, -0.22, 0.18) * drawn
    return jnp.clip(drawn, min=-limit, max=limit).astype(kind)


def setup_inputs(seed: int = 0) -> dict:
    keys = jax.random.split(jax.random.key(seed), 5)
    momentum = draw_momentum(jax.random.fold_in(keys[4], 71), 0)
    weight = scatter_about(keys[1], (ROWS, COLS), 1.0, 6.0, ((0, 32), (1, 16)))
    init_seed = jax.random.randint(keys[2], (1,), 0, 1000000).astype(jnp.int32)
    step_rate = jnp.clip(jnp.exp(jax.random.uniform(keys[3], (1,), jnp.float32, math.log(0.1), math.log(1.0))), 0.1, 1.0)
    return dict(momentum=momentum, weight=weight, init_seed=init_seed, step_rate=step_rate)


MOMENTUM_DECAY = 0.95
EPSILON = 1e-06

def hashed(flat_index, seed_value):
    mixed = flat_index * 747796405 + seed_value * 277803737 + 1013904223
    mixed = jnp.bitwise_xor(mixed, jnp.right_shift(mixed, 15))
    mixed = mixed * 1664525
    mixed = jnp.bitwise_xor(mixed, jnp.right_shift(mixed, 13))
    return (mixed % 65536).astype(jnp.float32) / 32768.0 - 1.0

def seed_block(seed_value, first_col, col_count, rank_count):
    columns = lax.iota(jnp.int32, col_count) + first_col
    flat_index = columns[:, None] * rank_count + lax.iota(jnp.int32, rank_count)[None, :]
    return hashed(flat_index, seed_value)

def reference(momentum, weight, init_seed, step_rate):
    highest = lax.Precision.HIGHEST
    start_factor = seed_block(init_seed[0], 0, COLS, RANK)
    projected = jnp.dot(momentum, start_factor, precision=highest)
    gram_matrix = jnp.dot(projected.T, projected, precision=highest)
    factor_low = jnp.linalg.cholesky(gram_matrix)
    ortho_basis = jax.scipy.linalg.solve_triangular(factor_low, projected.T, lower=True).T
    right_factor = jnp.dot(momentum.T, ortho_basis, precision=highest)
    scale = lax.rsqrt(lax.optimization_barrier(jnp.mean(right_factor * right_factor, axis=0)) + EPSILON)
    next_factor = (right_factor * scale[None, :]).T
    feedback = jnp.dot(ortho_basis, right_factor.T, precision=highest)
    momentum_next = momentum - (1.0 - MOMENTUM_DECAY) * feedback
    update = jnp.dot(ortho_basis, next_factor, precision=highest) * (ROWS / RANK) ** 0.5
    weight_next = (weight.astype(jnp.float32) - step_rate[0] * update).astype(jnp.bfloat16)
    return (momentum_next, weight_next, next_factor)
```

```python
import functools

import jax
import jax.numpy as jnp
from jax import lax
from jax.experimental import pallas as pl
from jax.experimental.pallas import tpu as pltpu
from jax.sharding import PartitionSpec as P

ROWS = 8192
COLS = 26624
RANK = 512
MOMENTUM_DECAY = 0.95
EPSILON = 1e-06
NX, NY, NZ = 4, 8, 8
TR, TC = 256, 1664
WIDE = 1280
NARROW = TC - WIDE
XS = RANK // NX
SL = XS // NY
YS = RANK // NY
HALF = TR // 2
PZ = HALF // NZ
F32, BF16, I32 = jnp.float32, jnp.bfloat16, jnp.int32
MESH = pl.DeviceIdType.MESH
HIGHEST = lax.Precision.HIGHEST
NN = (((1,), (0,)), ((), ()))
NT = (((1,), (1,)), ((), ()))
TN = (((0,), (0,)), ((), ()))


def split(value):
    high = value.astype(BF16)
    return high, (value - high.astype(F32)).astype(BF16)


def dot(left, right, dims=NN):
    return lax.dot_general(left, right, dims, preferred_element_type=F32)


def dot3(left, right, dims=NN):
    return dot(left[0], right[0], dims) + (dot(left[0], right[1], dims) + dot(left[1], right[0], dims))


def exact(left, right, dims=NN):
    return lax.dot_general(left, right, dims, precision=HIGHEST, preferred_element_type=F32)


def eliminate(first, last, block):
    lane = lax.broadcasted_iota(I32, (128, 128), 1)
    row_at = lax.broadcasted_iota(I32, (128, 128), 0)
    lane_one = lax.broadcasted_iota(I32, (1, 128), 1)

    def group(index, a):
        live = row_at < 128 - 8 * index
        for s in range(8):
            pivot = a[s : s + 1, s : s + 1]
            root = lax.rsqrt(pivot)
            root = root * (1.5 - 0.5 * pivot * root * root)
            row = jnp.where(lane_one == s, root, a[s : s + 1, :] * root)
            below = live & (row_at > s)
            factor = jnp.where(below, a[:, s : s + 1] * root, 0.0)
            a = jnp.where(lane == s, 0.0, a) - factor * row
            a = jnp.where(row_at == s, row, a)
        a = pltpu.roll(a, 120, 1)
        return jnp.concatenate([a[8:], a[:8]], axis=0)

    return lax.fori_loop(first, last, group, block)


def communicate(mom, seed, q_out, r_out, s_out, mh, ml, vh, vl, pp, ch, ph, zr, pf, pt, gp, gx, g1, gy, gs, gram, wp, xr, yr, bx, by, wt, acc,
                sq, sqr, sqc, sems_s, sems_r):
    r, c = lax.axis_index("row"), lax.axis_index("col")
    y, x, z, k = r // NX, r % NX, c // 2, c % 2
    used = [0]
    pending = []

    def peer(dx=0, dy=0, dz=0, dk=0):
        return (lax.rem(y + dy, NY) * NX + lax.rem(x + dx, NX), lax.rem(z + dz, NZ) * 2 + lax.rem(k + dk, 2))

    def send(src, dst, **where):
        slot = used[0]
        used[0] += 1
        copy = pltpu.make_async_remote_copy(
            src_ref=src, dst_ref=dst, send_sem=sems_s.at[slot], recv_sem=sems_r.at[slot], device_id=peer(**where), device_id_type=MESH
        )
        copy.start()
        pending.append(copy)
        return copy

    def sent(copy):
        copy.wait_send()
        pending[:] = [other for other in pending if other is not copy]

    xd, yd, zd = range(1, NX), range(1, NY), range(1, NZ)
    barrier = pltpu.get_barrier_semaphore()
    others = [dict(dk=1)] + [dict(dx=d) for d in xd] + [dict(dy=d) for d in yd] + [dict(dz=d) for d in zd]
    for where in others:
        pl.semaphore_signal(barrier, inc=1, device_id=peer(**where), device_id_type=MESH)

    rank_at = lax.broadcasted_iota(I32, (128, RANK), 0) * RANK + lax.broadcasted_iota(I32, (128, RANK), 1)
    base = rank_at * 747796405 + (seed[0] * 277803737 + 1013904223)

    @pl.loop(0, TC // 128)
    def _(part):
        mixed = base + (c * TC + part * 128) * (RANK * 747796405 % 2**32 - 2**32 * (RANK * 747796405 % 2**32 >= 2**31))
        mixed = jnp.bitwise_xor(mixed, jnp.right_shift(mixed, 15))
        mixed = mixed * 1664525
        mixed = jnp.bitwise_xor(mixed, jnp.right_shift(mixed, 13))
        value = jnp.bitwise_and(mixed, 65535).astype(F32) * (1.0 / 32768.0) - 1.0
        high, low = split(value)
        here = pl.ds(pl.multiple_of(part * 128, 128), 128)
        vh[here, :] = high
        vl[here, :] = low
        high, low = split(mom[:, here])
        mh[:, here] = high
        ml[:, here] = low

    for half in range(2):
        rows = slice(half * HALF, (half + 1) * HALF)
        pp[rows, :] = dot3((mh[rows, :], ml[rows, :]), (vh[...], vl[...]))
    pl.semaphore_wait(barrier, len(others))

    mine = pl.ds(pl.multiple_of(k * HALF, HALF), HALF)
    send(pp.at[pl.ds(pl.multiple_of((1 - k) * HALF, HALF), HALF)], ch, dk=1).wait_recv()
    ph[...] = pp[mine, :] + ch[...]
    copies = [send(ph.at[pl.ds(pl.multiple_of(lax.rem(z + d, NZ) * PZ, PZ), PZ)], zr.at[d - 1], dz=d) for d in zd]
    for copy in copies:
        copy.wait_recv()
    total = ph[pl.ds(pl.multiple_of(z * PZ, PZ), PZ), :]
    for d in zd:
        total = total + zr[d - 1]

    def p_rows(core, dz):
        return pl.ds(pl.multiple_of(core * HALF + lax.rem(z + dz, NZ) * PZ, PZ), PZ)

    pf[p_rows(k, 0), :] = total
    copies = [send(pf.at[p_rows(k, 0)], pf.at[p_rows(k, 0)], dz=d) for d in zd]
    siblings = [send(pf.at[p_rows(k, 0)], pf.at[p_rows(k, 0)], dk=1)]
    for d in zd:
        copies[d - 1].wait_recv()
        siblings.append(send(pf.at[p_rows(k, NZ - d)], pf.at[p_rows(k, NZ - d)], dk=1))
    for copy in siblings:
        copy.wait_recv()

    pt[...] = pf[...].T
    spot = k * 64 + z * 8
    for i in range(NX):
        gp[i * 8 : (i + 1) * 8, :] = pt[pl.ds(pl.multiple_of(i * XS + spot, 8), 8), :]
    gp2 = exact(gp[...], pf[...])
    gx[0] = gp2
    gcopies = [send(gx.at[0, pl.ds(pl.multiple_of(lax.rem(x + d, NX) * 8, 8), 8)], gx.at[d, pl.ds(0, 8)], dx=d) for d in xd]

    for i in range(NX):
        here = pl.ds(pl.multiple_of(i * XS, XS), XS)
        wp[here, :] = dot3(split(pt[here, :]), (mh[...], ml[...]))

    for copy in gcopies:
        copy.wait_recv()
    total = gx[0, pl.ds(pl.multiple_of(x * 8, 8), 8), :]
    for d in xd:
        total = total + gx[d, 0:8, :]
    g1[...] = total
    gcopies = [send(g1, gy.at[d - 1], dy=d) for d in yd]

    def a_rows(dx, dy):
        return pl.ds(pl.multiple_of(lax.rem(x + dx, NX) * XS + lax.rem(y + dy, NY) * SL, SL), SL)

    wide, narrow = pl.ds(0, WIDE), pl.ds(WIDE, NARROW)
    order = list(yd) + [0]
    xcopies = {}
    for e in order:
        for d in xd:
            xcopies[e, d] = send(wp.at[a_rows(d, e), wide], xr.at[d - 1, e], dx=d)

    def b_block(dy):
        return pl.ds(pl.multiple_of(lax.rem(y + dy, NY) * YS, YS), YS)

    for copy in gcopies:
        copy.wait_recv()
    total = g1[...]
    for d in yd:
        total = total + gy[d - 1]
    gs[pl.ds(pl.multiple_of(x * 8, 8), 8), :] = total
    own = pl.ds(pl.multiple_of(x * 8, 8), 8)
    gcopies = [send(gs.at[own], gs.at[own], dx=d) for d in xd]
    bcopies = [send(wp.at[b_block(d), narrow], by.at[d - 1], dy=d) for d in yd]
    for copy in gcopies:
        copy.wait_recv()

    def g_rows(i, core, dz):
        return pl.ds(pl.multiple_of(i * XS + core * 64 + lax.rem(z + dz, NZ) * 8, 8), 8)

    for i in range(NX):
        gram[g_rows(i, k, 0), :] = gs[i * 8 : (i + 1) * 8, :]
    zcopies = {}
    for i in range(NX):
        right = pl.ds(i * XS, RANK - i * XS)
        for d in zd:
            zcopies[i, d] = send(gram.at[g_rows(i, k, 0), right], gram.at[g_rows(i, k, 0), right], dz=d)
    scopies = []
    for i in range(NX):
        right = pl.ds(i * XS, RANK - i * XS)
        for d in zd:
            zcopies[i, d].wait_recv()
        rows = pl.ds(pl.multiple_of(i * XS + k * 64, 64), 64)
        scopies.append(send(gram.at[rows, right], gram.at[rows, right], dk=1))

    def wide_first(es):
        for e in es:
            for d in xd:
                xcopies[e, d].wait_recv()
            rows = a_rows(0, e)
            total = wp[rows, wide]
            for d in xd:
                total = total + xr[d - 1, e]
            wp[rows, wide] = total
            if e:
                ycopies[e] = send(wp.at[rows, wide], yr.at[e - 1], dy=e)

    def wide_second():
        for e in yd:
            ycopies[e].wait_recv()
        rows = a_rows(0, 0)
        total = wp[rows, wide]
        for e in yd:
            total = total + yr[e - 1]
        wt[rows, wide] = total
        for e in yd:
            agy[e] = send(wt.at[rows, wide], wt.at[rows, wide], dy=e)
        for d in xd:
            agx.append(send(wt.at[rows, wide], wt.at[rows, wide], dx=d))

    def wide_third(es):
        for e in es:
            agy[e].wait_recv()
            rows = a_rows(0, NY - e)
            for d in xd:
                agx.append(send(wt.at[rows, wide], wt.at[rows, wide], dx=d))

    def b_rows(dx):
        return pl.ds(pl.multiple_of(y * YS + lax.rem(x + dx, NX) * SL, SL), SL)

    def narrow_first():
        for copy in bcopies:
            copy.wait_recv()
        rows = b_block(0)
        total = wp[rows, narrow]
        for e in yd:
            total = total + by[e - 1]
        wp[rows, narrow] = total
        for d in xd:
            bxc.append(send(wp.at[b_rows(d), narrow], bx.at[d - 1], dx=d))

    def narrow_second():
        for copy in bxc:
            copy.wait_recv()
        rows = b_rows(0)
        total = wp[rows, narrow]
        for d in xd:
            total = total + bx[d - 1]
        wt[rows, narrow] = total
        for d in xd:
            bgx.append(send(wt.at[rows, narrow], wt.at[rows, narrow], dx=d))

    def narrow_third():
        for copy in bgx:
            copy.wait_recv()
        for e in yd:
            bgy.append(send(wt.at[b_block(0), narrow], wt.at[b_block(0), narrow], dy=e))

    ycopies, agy, agx, bxc, bgx, bgy = {}, {}, [], [], [], []
    between = [
        lambda: wide_first((1, 2, 3)),
        lambda: (wide_first((4, 5, 6, 7, 0)), narrow_first()),
        lambda: narrow_second(),
        lambda: (wide_second(), narrow_third()),
        lambda: wide_third((1, 7, 2)),
        lambda: wide_third((6, 3, 5)),
        lambda: wide_third((4,)),
        lambda: None,
    ]

    scopies[0].wait_recv()

    for b in range(NX):
        low, high = b * XS, (b + 1) * XS
        block = eliminate(0, 8, gram[low:high, low:high])
        between[2 * b]()
        block = eliminate(8, 16, block)
        between[2 * b + 1]()
        if b == 0:
            for copy in scopies[1:]:
                copy.wait_recv()
            for copy in list(zcopies.values()) + scopies:
                sent(copy)
        panel = exact(block, gram[low:high, :])
        gram[low:high, :] = panel
        gram[low:high, low:high] = block
        if b < NX - 1:
            factor = gram[low:high, high:].T
            cross = exact(factor, gram[low:high, :])
            old = gram[high:, :]
            spot_lane = lax.broadcasted_iota(I32, (RANK - high, RANK), 1)
            gram[high:, :] = jnp.where((spot_lane >= low) & (spot_lane < high), 0.0, old) - cross

    inverse = gram
    q_in = split(pf[...])
    for b in range(NX):
        high = (b + 1) * XS
        q_out[:, b * XS : high] = dot3((q_in[0][:, :high], q_in[1][:, :high]), split(inverse[b * XS : high, :high]), NT)

    for copy in agx + bgy:
        copy.wait_recv()
    factors = [split(inverse[b * XS : (b + 1) * XS, : (b + 1) * XS]) for b in range(NX)]
    acc[...] = jnp.zeros_like(acc)

    @pl.loop(0, TC // 128)
    def _(part):
        here = pl.ds(pl.multiple_of(part * 128, 128), 128)
        high, low = split(wt[:, here])
        for b in range(NX):
            end = (b + 1) * XS
            rows = slice(b * XS, end)
            piece = dot3(factors[b], (high[:end], low[:end]))
            r_out[rows, here] = piece
            acc[rows, :] += piece * piece

    sub = lax.broadcasted_iota(I32, (8, 128), 0)
    packed = jnp.zeros((8, 128), F32)
    for b in range(NX):
        packed = jnp.where(sub == b, exact(jnp.ones((8, 128), F32), acc[b * XS : (b + 1) * XS, :], NT), packed)
    sq[...] = packed
    copies = [send(sq, sqr.at[d - 1], dz=d) for d in zd]
    for copy in copies:
        copy.wait_recv()
    for d in zd:
        packed = packed + sqr[d - 1]
    sqc[0] = packed
    send(sqc.at[0], sqc.at[1], dk=1).wait_recv()
    s_out[...] = lax.rsqrt((sqc[0] + sqc[1]) * (1.0 / COLS) + EPSILON)
    for copy in pending:
        copy.wait_send()


SENDS = 1 + 7 + 7 + 8 + 3 + 7 + 24 + 3 + 7 + 28 + 4 + 7 + 7 + 24 + 3 + 3 + 7 + 7 + 1


def outputs(mom, weight, q, r, s, rate, mom_out, weight_out):
    sub = lax.broadcasted_iota(I32, (8, 128), 0)
    scales = jnp.concatenate([jnp.sum(jnp.where(sub == b, s[...], 0.0), axis=0, keepdims=True) for b in range(NX)], axis=1)
    basis = q[...]
    right = split(r[...])
    feedback = dot(basis.astype(BF16), right[0])
    update = dot3(split(basis * scales), right) * (ROWS / RANK) ** 0.5
    mom_out[...] = mom[...] - (1.0 - MOMENTUM_DECAY) * feedback
    weight_out[...] = (weight[...].astype(F32) - rate[0] * update).astype(BF16)


def per_device(momentum, weight, init_seed, step_rate):
    vmem, smem = pl.BlockSpec(memory_space=pltpu.VMEM), pl.BlockSpec(memory_space=pltpu.SMEM)
    q, right, scales = pl.pallas_call(
        communicate,
        out_shape=[jax.ShapeDtypeStruct((TR, RANK), F32), jax.ShapeDtypeStruct((RANK, TC), F32), jax.ShapeDtypeStruct((8, 128), F32)],
        in_specs=[vmem, smem],
        out_specs=[vmem, vmem, vmem],
        scratch_shapes=[
            pltpu.VMEM((TR, TC), BF16),
            pltpu.VMEM((TR, TC), BF16),
            pltpu.VMEM((TC, RANK), BF16),
            pltpu.VMEM((TC, RANK), BF16),
            pltpu.VMEM((TR, RANK), F32),
            pltpu.VMEM((HALF, RANK), F32),
            pltpu.VMEM((HALF, RANK), F32),
            pltpu.VMEM((NZ - 1, PZ, RANK), F32),
            pltpu.VMEM((TR, RANK), F32),
            pltpu.VMEM((RANK, TR), F32),
            pltpu.VMEM((32, TR), F32),
            pltpu.VMEM((NX, 32, RANK), F32),
            pltpu.VMEM((8, RANK), F32),
            pltpu.VMEM((NY - 1, 8, RANK), F32),
            pltpu.VMEM((32, RANK), F32),
            pltpu.VMEM((RANK, RANK), F32),
            pltpu.VMEM((RANK, TC), F32),
            pltpu.VMEM((NX - 1, NY, SL, WIDE), F32),
            pltpu.VMEM((NY - 1, SL, WIDE), F32),
            pltpu.VMEM((NX - 1, SL, NARROW), F32),
            pltpu.VMEM((NY - 1, YS, NARROW), F32),
            pltpu.VMEM((RANK, TC), F32),
            pltpu.VMEM((RANK, 128), F32),
            pltpu.VMEM((8, 128), F32),
            pltpu.VMEM((NZ - 1, 8, 128), F32),
            pltpu.VMEM((2, 8, 128), F32),
            pltpu.SemaphoreType.DMA((SENDS,)),
            pltpu.SemaphoreType.DMA((SENDS,)),
        ],
        compiler_params=pltpu.CompilerParams(collective_id=0, has_side_effects=True, vmem_limit_bytes=56 * 2**20),
        name="communicate",
    )(momentum, init_seed)
    tile = pl.BlockSpec((TR, 128), lambda i: (0, i))
    momentum_next, weight_next = pl.pallas_call(
        outputs,
        grid=(TC // 128,),
        out_shape=[jax.ShapeDtypeStruct((TR, TC), F32), jax.ShapeDtypeStruct((TR, TC), BF16)],
        in_specs=[
            tile,
            tile,
            pl.BlockSpec((TR, RANK), lambda i: (0, 0)),
            pl.BlockSpec((RANK, 128), lambda i: (0, i)),
            pl.BlockSpec((8, 128), lambda i: (0, 0)),
            smem,
        ],
        out_specs=[tile, tile],
        compiler_params=pltpu.CompilerParams(vmem_limit_bytes=40 * 2**20),
        name="outputs",
    )(momentum, weight, q, right, scales, step_rate)
    begin = lax.axis_index("row") * SL
    scale_here = lax.dynamic_slice_in_dim(scales[:NX].reshape(RANK), begin, SL, 0)
    next_factor = lax.dynamic_slice_in_dim(right, begin, SL, 0) * scale_here[:, None]
    return (momentum_next, weight_next, next_factor)


def solution(mesh):
    placed = (P("row", "col"), P("row", "col"), P(), P())
    return jax.shard_map(
        per_device,
        mesh=mesh,
        in_specs=placed,
        out_specs=(P("row", "col"), P("row", "col"), P("row", "col")),
        check_vma=False,
    )
```

```python
import functools

import jax
import jax.numpy as jnp
from jax import lax
from jax.experimental import pallas as pl
from jax.experimental.pallas import tpu as pltpu
from jax.sharding import PartitionSpec as P

ROWS = 8192
COLS = 26624
RANK = 512
MOMENTUM_DECAY = 0.95
EPSILON = 1e-06
NX, NY, NZ = 4, 8, 8
TR, TC = 256, 1664
WIDE = 1024
NARROW = TC - WIDE
LEFT = 384
XS = RANK // NX
SL = XS // NY
YS = RANK // NY
HALF = TR // 2
PARTS = ((0, 512), (512, 512), (1024, 640))
PZ = HALF // NZ
F32, BF16, I32 = jnp.float32, jnp.bfloat16, jnp.int32
MESH = pl.DeviceIdType.MESH
HIGHEST = lax.Precision.HIGHEST
NN = (((1,), (0,)), ((), ()))
NT = (((1,), (1,)), ((), ()))
TN = (((0,), (0,)), ((), ()))


def split(value):
    high = value.astype(BF16)
    return high, (value - high.astype(F32)).astype(BF16)


def dot(left, right, dims=NN):
    return lax.dot_general(left, right, dims, preferred_element_type=F32)


def dot3(left, right, dims=NN):
    return dot(left[0], right[0], dims) + (dot(left[0], right[1], dims) + dot(left[1], right[0], dims))


def exact(left, right, dims=NN):
    return lax.dot_general(left, right, dims, precision=HIGHEST, preferred_element_type=F32)


def eliminate(tiles, groups):
    lane = lax.broadcasted_iota(I32, (8, 128), 1)
    sub = lax.broadcasted_iota(I32, (8, 128), 0)

    def spread(value):
        return jnp.broadcast_to(value, (8, 128))

    for q in groups:
        o = 8 * q
        top = tiles[q]
        columns = [spread(top[:, o + s : o + s + 1]) for s in range(8)]
        item = {(s, t): spread(columns[s][t : t + 1, :]) for s in range(8) for t in range(s, 8)}
        rows = [spread(top[s : s + 1, :]) for s in range(8)]
        lower, roots, done = {}, [], []
        for s in range(8):
            root = lax.rsqrt(item[s, s])
            roots.append(root)
            for t in range(s + 1, 8):
                lower[t, s] = item[s, t] * root
            for t in range(s + 1, 8):
                for u in range(t, 8):
                    item[t, u] = item[t, u] - lower[t, s] * lower[u, s]
            full = jnp.where(lane == o + s, root, rows[s] * root)
            for t in range(s + 1, 8):
                rows[t] = jnp.where(lane == o + s, 0.0, rows[t]) - lower[t, s] * full
            done.append(jnp.where((lane > o + s) & (lane < o + 8), 0.0, full))
        new = done[0]
        for s in range(1, 8):
            new = jnp.where(sub == s, done[s], new)
        tiles[q] = new
        here = (lane >= o) & (lane < o + 8)
        for i in range(16):
            if i < q:
                tiles[i] = jnp.where(here, 0.0, tiles[i])
            if i > q:
                rest = jnp.where(here, 0.0, tiles[i])
                factors = []
                for s in range(8):
                    factor = spread(tiles[i][:, o + s : o + s + 1])
                    for u in range(s):
                        factor = factor - factors[u] * lower[s, u]
                    factor = factor * roots[s]
                    factors.append(factor)
                    rest = rest - factor * done[s]
                tiles[i] = rest


def update_tile(mom, weight_in, seed, rate, mom_out, weight_out, next_out, w_in, mom_new, w_new, next_new, qb, rt, rh, rl, mh, ml, vh, vl, pp, ch, ph, zr, pf, pt, gp, gx, g1, gy, gs, gram, wp, xr, yr, bx, by, wt,
                sq, sqr, sqc, sems_s, sems_r, sems_l):
    r, c = lax.axis_index("row"), lax.axis_index("col")
    y, x, z, k = r // NX, r % NX, c // 2, c % 2
    used = [0]
    pending = []

    def peer(dx=0, dy=0, dz=0, dk=0):
        return (lax.rem(y + dy, NY) * NX + lax.rem(x + dx, NX), lax.rem(z + dz, NZ) * 2 + lax.rem(k + dk, 2))

    def send(src, dst, **where):
        slot = used[0]
        used[0] += 1
        copy = pltpu.make_async_remote_copy(
            src_ref=src, dst_ref=dst, send_sem=sems_s.at[slot], recv_sem=sems_r.at[slot], device_id=peer(**where), device_id_type=MESH
        )
        copy.start()
        pending.append(copy)
        return copy

    def sent(copy):
        copy.wait_send()
        pending[:] = [other for other in pending if other is not copy]

    xd, yd, zd = range(1, NX), range(1, NY), range(1, NZ)
    barrier = pltpu.get_barrier_semaphore()
    others = [dict(dk=1)] + [dict(dx=d) for d in xd] + [dict(dy=d) for d in yd] + [dict(dz=d) for d in zd]
    for where in others:
        pl.semaphore_signal(barrier, inc=1, device_id=peer(**where), device_id_type=MESH)

    weight_copy = pltpu.make_async_copy(weight_in, w_in, sems_l.at[0])
    weight_copy.start()

    rank_at = lax.broadcasted_iota(I32, (128, RANK), 0) * RANK + lax.broadcasted_iota(I32, (128, RANK), 1)
    base = rank_at * 747796405 + (seed[0] * 277803737 + 1013904223)

    @pl.loop(0, TC // 128)
    def _(part):
        mixed = base + (c * TC + part * 128) * (RANK * 747796405 % 2**32 - 2**32 * (RANK * 747796405 % 2**32 >= 2**31))
        mixed = jnp.bitwise_xor(mixed, jnp.right_shift(mixed, 15))
        mixed = mixed * 1664525
        mixed = jnp.bitwise_xor(mixed, jnp.right_shift(mixed, 13))
        value = jnp.bitwise_and(mixed, 65535).astype(F32) * (1.0 / 32768.0) - 1.0
        high, low = split(value)
        here = pl.ds(pl.multiple_of(part * 128, 128), 128)
        vh[here, :] = high
        vl[here, :] = low
        high, low = split(mom[:, here])
        mh[:, here] = high
        ml[:, here] = low

    for half in range(2):
        rows = slice(half * HALF, (half + 1) * HALF)
        pp[rows, :] = dot3((mh[rows, :], ml[rows, :]), (vh[...], vl[...]))
    pl.semaphore_wait(barrier, len(others))

    mine = pl.ds(pl.multiple_of(k * HALF, HALF), HALF)
    send(pp.at[pl.ds(pl.multiple_of((1 - k) * HALF, HALF), HALF)], ch, dk=1).wait_recv()
    ph[...] = pp[mine, :] + ch[...]
    copies = [send(ph.at[pl.ds(pl.multiple_of(lax.rem(z + d, NZ) * PZ, PZ), PZ)], zr.at[d - 1], dz=d) for d in zd]
    for copy in copies:
        copy.wait_recv()
    total = ph[pl.ds(pl.multiple_of(z * PZ, PZ), PZ), :]
    for d in zd:
        total = total + zr[d - 1]

    def p_rows(core, dz):
        return pl.ds(pl.multiple_of(core * HALF + lax.rem(z + dz, NZ) * PZ, PZ), PZ)

    pf[p_rows(k, 0), :] = total
    copies = [send(pf.at[p_rows(k, 0)], pf.at[p_rows(k, 0)], dz=d) for d in zd]
    siblings = [send(pf.at[p_rows(k, 0)], pf.at[p_rows(k, 0)], dk=1)]
    for d in zd:
        copies[d - 1].wait_recv()
        siblings.append(send(pf.at[p_rows(k, NZ - d)], pf.at[p_rows(k, NZ - d)], dk=1))
    for copy in siblings:
        copy.wait_recv()

    pt[...] = pf[...].T
    spot = k * 64 + z * 8
    for i in range(NX):
        gp[i * 8 : (i + 1) * 8, :] = pt[pl.ds(pl.multiple_of(i * XS + spot, 8), 8), :]
    gp2 = exact(gp[...], pf[...])
    gx[0] = gp2
    gcopies = [send(gx.at[0, pl.ds(pl.multiple_of(lax.rem(x + d, NX) * 8, 8), 8)], gx.at[d, pl.ds(0, 8)], dx=d) for d in xd]

    for i in range(NX):
        here = pl.ds(pl.multiple_of(i * XS, XS), XS)
        wp[here, :] = dot3(split(pt[here, :]), (mh[...], ml[...]))

    wide, narrow = pl.ds(0, WIDE), pl.ds(WIDE, NARROW)
    left, right_half = pl.ds(WIDE, LEFT), pl.ds(WIDE + LEFT, NARROW - LEFT)

    def a_rows(dx, dy):
        return pl.ds(pl.multiple_of(lax.rem(x + dx, NX) * XS + lax.rem(y + dy, NY) * SL, SL), SL)

    def b_block(dy):
        return pl.ds(pl.multiple_of(lax.rem(y + dy, NY) * YS, YS), YS)

    def b_rows(dx):
        return pl.ds(pl.multiple_of(y * YS + lax.rem(x + dx, NX) * SL, SL), SL)

    xcopies, ycopies, agy, agx, bup, bdown, bxc, bgx, bgup, bgdown = {}, {}, {}, [], {}, {}, [], [], {}, {}

    def wide_start(es):
        for e in es:
            for d in xd:
                xcopies[e, d] = send(wp.at[a_rows(d, e), wide], xr.at[d - 1, e], dx=d)

    def wide_first(e):
        for d in xd:
            xcopies[e, d].wait_recv()
        rows = a_rows(0, e)
        total = wp[rows, wide]
        for d in xd:
            total = total + xr[d - 1, e]
        wp[rows, wide] = total
        if e:
            ycopies[e] = send(wp.at[rows, wide], yr.at[e - 1], dy=e)

    def wide_second():
        for e in yd:
            ycopies[e].wait_recv()
        rows = a_rows(0, 0)
        total = wp[rows, wide]
        for e in yd:
            total = total + yr[e - 1]
        wt[rows, wide] = total
        for d in xd:
            agx.append(send(wt.at[rows, wide], wt.at[rows, wide], dx=d))
        for e in (1, 7, 2, 6, 3, 5, 4):
            agy[e] = send(wt.at[rows, wide], wt.at[rows, wide], dy=e)

    def wide_third(e):
        agy[e].wait_recv()
        rows = a_rows(0, NY - e)
        for d in xd:
            agx.append(send(wt.at[rows, wide], wt.at[rows, wide], dx=d))

    def narrow_start():
        bup[4] = send(wp.at[b_block(4), left], by.at[0, :, pl.ds(0, LEFT)], dy=1)
        bdown[4] = send(wp.at[b_block(4), right_half], by.at[4, :, pl.ds(LEFT, NARROW - LEFT)], dy=NY - 1)

    def narrow_step(d):
        bup[d + 1].wait_recv()
        bdown[d + 1].wait_recv()
        if d == 3:
            wp[b_block(3), left] += by[0, :, 0:LEFT]
            wp[b_block(5), right_half] += by[4, :, LEFT:NARROW]
        else:
            wp[b_block(d), narrow] += by[3 - d]
            wp[b_block(NY - d), narrow] += by[7 - d]
        bup[d] = send(wp.at[b_block(d), narrow], by.at[4 - d], dy=1)
        bdown[d] = send(wp.at[b_block(NY - d), narrow], by.at[8 - d], dy=NY - 1)

    def narrow_first():
        bup[1].wait_recv()
        bdown[1].wait_recv()
        wp[b_block(0), narrow] += by[3] + by[7]
        for d in xd:
            bxc.append(send(wp.at[b_rows(d), narrow], bx.at[d - 1], dx=d))

    def narrow_second():
        for copy in bxc:
            copy.wait_recv()
        rows = b_rows(0)
        total = wp[rows, narrow]
        for d in xd:
            total = total + bx[d - 1]
        wt[rows, narrow] = total
        for d in xd:
            bgx.append(send(wt.at[rows, narrow], wt.at[rows, narrow], dx=d))

    def narrow_gather(d):
        if d == 0:
            for copy in bgx:
                copy.wait_recv()
        else:
            bgup[d - 1].wait_recv()
            bgdown[d - 1].wait_recv()
        up, down = (left, right_half) if d == 3 else (narrow, narrow)
        bgup[d] = send(wt.at[b_block(NY - d if d else 0), up], wt.at[b_block(NY - d if d else 0), up], dy=1)
        bgdown[d] = send(wt.at[b_block(d), down], wt.at[b_block(d), down], dy=NY - 1)

    for copy in gcopies:
        copy.wait_recv()
    total = gx[0, pl.ds(pl.multiple_of(x * 8, 8), 8), :]
    for d in xd:
        total = total + gx[d, 0:8, :]
    g1[...] = total
    gcopies = [send(g1, gy.at[d - 1], dy=d) for d in yd]
    wide_start((1, 2, 3))
    narrow_start()
    for copy in gcopies:
        copy.wait_recv()
    total = g1[...]
    for d in yd:
        total = total + gy[d - 1]
    own = pl.ds(pl.multiple_of(x * 8, 8), 8)
    gs[own, :] = total
    gcopies = [send(gs.at[own], gs.at[own], dx=d) for d in xd]
    wide_start((4, 5, 6, 7, 0))
    narrow_step(3)
    wide_first(1)
    for copy in gcopies:
        copy.wait_recv()

    def g_rows(i, core, dz):
        return pl.ds(pl.multiple_of(i * XS + core * 64 + lax.rem(z + dz, NZ) * 8, 8), 8)

    for i in range(NX):
        gram[g_rows(i, k, 0), :] = gs[i * 8 : (i + 1) * 8, :]
    zcopies = {}
    for i in range(NX):
        right = pl.ds(i * XS, RANK - i * XS)
        for d in zd:
            zcopies[i, d] = send(gram.at[g_rows(i, k, 0), right], gram.at[g_rows(i, k, 0), right], dz=d)
    wide_first(2)
    narrow_step(2)
    wide_first(3)
    scopies = []
    for i in range(NX):
        right = pl.ds(i * XS, RANK - i * XS)
        for d in zd:
            zcopies[i, d].wait_recv()
        rows = pl.ds(pl.multiple_of(i * XS + k * 64, 64), 64)
        scopies.append(send(gram.at[rows, right], gram.at[rows, right], dk=1))
    scopies[0].wait_recv()

    jobs = [
        [lambda: wide_first(4), lambda: narrow_step(1)],
        [lambda: wide_first(5)],
        [lambda: wide_first(6)],
        [lambda: narrow_first(), lambda: wide_first(7)],
        [],
        [lambda: narrow_second(), lambda: wide_first(0)],
        [],
        [lambda: narrow_gather(0), lambda: wide_second()],
        [],
        [lambda: narrow_gather(1)],
        [lambda: wide_third(1), lambda: wide_third(7)],
        [],
        [lambda: wide_third(2), lambda: wide_third(6)],
        [lambda: narrow_gather(2)],
        [lambda: wide_third(3), lambda: wide_third(5)],
        [lambda: wide_third(4), lambda: narrow_gather(3)],
    ]

    for b in range(NX):
        low, high = b * XS, (b + 1) * XS
        tiles = [gram[low + 8 * i : low + 8 * i + 8, low:high] for i in range(16)]
        for part in range(4):
            eliminate(tiles, range(4 * part, 4 * part + 4))
            for job in jobs[4 * b + part]:
                job()
        block = jnp.concatenate(tiles, axis=0)
        if b == 0:
            for copy in scopies[1:]:
                copy.wait_recv()
            for copy in list(zcopies.values()) + scopies:
                sent(copy)
        panel = exact(block, gram[low:high, :])
        gram[low:high, :] = panel
        gram[low:high, low:high] = block
        if b < NX - 1:
            factor = gram[low:high, high:].T
            cross = exact(factor, gram[low:high, :])
            old = gram[high:, :]
            spot_lane = lax.broadcasted_iota(I32, (RANK - high, RANK), 1)
            gram[high:, :] = jnp.where((spot_lane >= low) & (spot_lane < high), 0.0, old) - cross

    inverse = gram
    q_in = split(pf[...])
    for b in range(NX):
        high = (b + 1) * XS
        qb[:, b * XS : high] = dot3((q_in[0][:, :high], q_in[1][:, :high]), split(inverse[b * XS : high, :high]), NT)

    for copy in agx + [bgup[3], bgdown[3]]:
        copy.wait_recv()
    factors = [split(inverse[b * XS : (b + 1) * XS, : (b + 1) * XS]) for b in range(NX)]
    squares = [jnp.zeros((XS, 128), F32) for _ in range(NX)]
    for begin, count in PARTS:
        here = slice(begin, begin + count)
        high, low = split(wt[:, here])
        for b in range(NX):
            end = (b + 1) * XS
            rows = slice(b * XS, end)
            piece = dot3(factors[b], (high[:end], low[:end]))
            rt[rows, here] = piece
            for i in range(count // 128):
                squares[b] += piece[:, i * 128 : (i + 1) * 128] ** 2

    sub = lax.broadcasted_iota(I32, (8, 128), 0)
    packed = jnp.zeros((8, 128), F32)
    for b in range(NX):
        packed = jnp.where(sub == b, exact(jnp.ones((8, 128), F32), squares[b], NT), packed)
    sq[...] = packed
    copies = [send(sq, sqr.at[d - 1], dz=d) for d in zd]

    basis = qb[...].astype(BF16)
    for begin, count in PARTS:
        here = slice(begin, begin + count)
        high, low = split(rt[:, here])
        rh[:, here] = high
        rl[:, here] = low
        mom_new[:, here] = mom[:, here] - (1.0 - MOMENTUM_DECAY) * dot(basis, high)
    mom_copy = pltpu.make_async_copy(mom_new, mom_out, sems_l.at[1])
    mom_copy.start()
    for copy in copies:
        copy.wait_recv()
    for d in zd:
        packed = packed + sqr[d - 1]
    sqc[0] = packed
    send(sqc.at[0], sqc.at[1], dk=1).wait_recv()
    scales = lax.rsqrt((sqc[0] + sqc[1]) * (1.0 / COLS) + EPSILON)

    scale_row = jnp.concatenate([scales[b : b + 1, :] for b in range(NX)], axis=1)
    weight_copy.wait()
    scaled = split(qb[...] * (scale_row * (ROWS / RANK) ** 0.5))
    for begin, count in PARTS:
        here = slice(begin, begin + count)
        update = dot3(scaled, (rh[:, here], rl[:, here]))
        w_new[:, here] = (w_in[:, here].astype(F32) - rate[0] * update).astype(BF16)
    weight_out_copy = pltpu.make_async_copy(w_new, weight_out, sems_l.at[2])
    weight_out_copy.start()
    picked = lax.broadcasted_iota(I32, (SL, RANK), 1) == r * SL + lax.broadcasted_iota(I32, (SL, RANK), 0)
    own_scale = jnp.sum(jnp.where(picked, scale_row, 0.0), axis=1, keepdims=True)
    next_new[...] = rt[pl.ds(pl.multiple_of(r * SL, SL), SL), :] * own_scale
    next_copy = pltpu.make_async_copy(next_new, next_out, sems_l.at[3])
    next_copy.start()
    mom_copy.wait()
    weight_out_copy.wait()
    next_copy.wait()
    for copy in pending:
        copy.wait_send()


SENDS = 1 + 7 + 7 + 8 + 3 + 7 + 24 + 3 + 28 + 4 + 7 + 7 + 24 + 8 + 3 + 3 + 8 + 7 + 1


def per_device(momentum, weight, init_seed, step_rate):
    vmem, smem, anywhere = (pl.BlockSpec(memory_space=space) for space in (pltpu.VMEM, pltpu.SMEM, pl.ANY))
    return pl.pallas_call(
        update_tile,
        out_shape=[
            jax.ShapeDtypeStruct((TR, TC), F32),
            jax.ShapeDtypeStruct((TR, TC), BF16),
            jax.ShapeDtypeStruct((SL, TC), F32),
        ],
        in_specs=[vmem, anywhere, smem, smem],
        out_specs=[anywhere, anywhere, anywhere],
        scratch_shapes=[
            pltpu.VMEM((TR, TC), BF16),
            pltpu.VMEM((TR, TC), F32),
            pltpu.VMEM((TR, TC), BF16),
            pltpu.VMEM((SL, TC), F32),
            pltpu.VMEM((TR, RANK), F32),
            pltpu.VMEM((RANK, TC), F32),
            pltpu.VMEM((RANK, TC), BF16),
            pltpu.VMEM((RANK, TC), BF16),
            pltpu.VMEM((TR, TC), BF16),
            pltpu.VMEM((TR, TC), BF16),
            pltpu.VMEM((TC, RANK), BF16),
            pltpu.VMEM((TC, RANK), BF16),
            pltpu.VMEM((TR, RANK), F32),
            pltpu.VMEM((HALF, RANK), F32),
            pltpu.VMEM((HALF, RANK), F32),
            pltpu.VMEM((NZ - 1, PZ, RANK), F32),
            pltpu.VMEM((TR, RANK), F32),
            pltpu.VMEM((RANK, TR), F32),
            pltpu.VMEM((32, TR), F32),
            pltpu.VMEM((NX, 32, RANK), F32),
            pltpu.VMEM((8, RANK), F32),
            pltpu.VMEM((NY - 1, 8, RANK), F32),
            pltpu.VMEM((32, RANK), F32),
            pltpu.VMEM((RANK, RANK), F32),
            pltpu.VMEM((RANK, TC), F32),
            pltpu.VMEM((NX - 1, NY, SL, WIDE), F32),
            pltpu.VMEM((NY - 1, SL, WIDE), F32),
            pltpu.VMEM((NX - 1, SL, NARROW), F32),
            pltpu.VMEM((8, YS, NARROW), F32),
            pltpu.VMEM((RANK, TC), F32),
            pltpu.VMEM((8, 128), F32),
            pltpu.VMEM((NZ - 1, 8, 128), F32),
            pltpu.VMEM((2, 8, 128), F32),
            pltpu.SemaphoreType.DMA((SENDS,)),
            pltpu.SemaphoreType.DMA((SENDS,)),
            pltpu.SemaphoreType.DMA((4,)),
        ],
        compiler_params=pltpu.CompilerParams(collective_id=0, has_side_effects=True, vmem_limit_bytes=56 * 2**20),
        name="update_tile",
    )(momentum, weight, init_seed, step_rate)


def solution(mesh):
    placed = (P("row", "col"), P("row", "col"), P(), P())
    return jax.shard_map(
        per_device,
        mesh=mesh,
        in_specs=placed,
        out_specs=(P("row", "col"), P("row", "col"), P("row", "col")),
        check_vma=False,
    )
```

```python
import functools

import jax
import jax.numpy as jnp
from jax import lax
from jax.experimental import pallas as pl
from jax.experimental.pallas import tpu as pltpu
from jax.sharding import PartitionSpec as P

ROWS = 8192
COLS = 26624
RANK = 512
MOMENTUM_DECAY = 0.95
EPSILON = 1e-06
NX, NY, NZ = 4, 8, 8
TR, TC = 256, 1664
WIDE = 1024
NARROW = TC - WIDE
HW = WIDE // 2
CHUNKS = ((0, 256, (4, 3)), (256, 256, (3, 4)), (512, 128, (4, 3)))
XS = RANK // NX
SL = XS // NY
YS = RANK // NY
HALF = TR // 2
PARTS = ((0, 512), (512, 512), (1024, 640))
PZ = HALF // NZ
F32, BF16, I32 = jnp.float32, jnp.bfloat16, jnp.int32
MESH = pl.DeviceIdType.MESH
HIGHEST = lax.Precision.HIGHEST
NN = (((1,), (0,)), ((), ()))
NT = (((1,), (1,)), ((), ()))
TN = (((0,), (0,)), ((), ()))


def split(value):
    high = value.astype(BF16)
    return high, (value - high.astype(F32)).astype(BF16)


def dot(left, right, dims=NN):
    return lax.dot_general(left, right, dims, preferred_element_type=F32)


def dot3(left, right, dims=NN):
    return dot(left[0], right[0], dims) + (dot(left[0], right[1], dims) + dot(left[1], right[0], dims))


def exact(left, right, dims=NN):
    return lax.dot_general(left, right, dims, precision=HIGHEST, preferred_element_type=F32)


def eliminate(tiles, groups):
    lane = lax.broadcasted_iota(I32, (8, 128), 1)
    sub = lax.broadcasted_iota(I32, (8, 128), 0)

    def spread(value):
        return jnp.broadcast_to(value, (8, 128))

    for q in groups:
        o = 8 * q
        top = tiles[q]
        columns = [spread(top[:, o + s : o + s + 1]) for s in range(8)]
        item = {(s, t): spread(columns[s][t : t + 1, :]) for s in range(8) for t in range(s, 8)}
        rows = [spread(top[s : s + 1, :]) for s in range(8)]
        lower, roots, done = {}, [], []
        for s in range(8):
            root = lax.rsqrt(item[s, s])
            roots.append(root)
            for t in range(s + 1, 8):
                lower[t, s] = item[s, t] * root
            for t in range(s + 1, 8):
                for u in range(t, 8):
                    item[t, u] = item[t, u] - lower[t, s] * lower[u, s]
            full = jnp.where(lane == o + s, root, rows[s] * root)
            for t in range(s + 1, 8):
                rows[t] = jnp.where(lane == o + s, 0.0, rows[t]) - lower[t, s] * full
            done.append(jnp.where((lane > o + s) & (lane < o + 8), 0.0, full))
        new = done[0]
        for s in range(1, 8):
            new = jnp.where(sub == s, done[s], new)
        tiles[q] = new
        here = (lane >= o) & (lane < o + 8)
        for i in range(16):
            if i < q:
                tiles[i] = jnp.where(here, 0.0, tiles[i])
            if i > q:
                rest = jnp.where(here, 0.0, tiles[i])
                factors = []
                for s in range(8):
                    factor = spread(tiles[i][:, o + s : o + s + 1])
                    for u in range(s):
                        factor = factor - factors[u] * lower[s, u]
                    factor = factor * roots[s]
                    factors.append(factor)
                    rest = rest - factor * done[s]
                tiles[i] = rest


def update_tile(mom, weight_in, seed, rate, mom_out, weight_out, next_out, w_in, mom_new, w_new, next_new, qb, rt, rh, rl, mh, ml, vh, vl, pp, ch, ph, zr, pf, pt, gp, gx, g1, gy, gs, gram, wp, xr, yr, bx, by, wt,
                sq, sqr, sqc, sems_s, sems_r, sems_l):
    r, c = lax.axis_index("row"), lax.axis_index("col")
    y, x, z, k = r // NX, r % NX, c // 2, c % 2
    used = [0]
    pending = []

    def peer(dx=0, dy=0, dz=0, dk=0):
        return (lax.rem(y + dy, NY) * NX + lax.rem(x + dx, NX), lax.rem(z + dz, NZ) * 2 + lax.rem(k + dk, 2))

    def send(src, dst, **where):
        slot = used[0]
        used[0] += 1
        copy = pltpu.make_async_remote_copy(
            src_ref=src, dst_ref=dst, send_sem=sems_s.at[slot], recv_sem=sems_r.at[slot], device_id=peer(**where), device_id_type=MESH
        )
        copy.start()
        pending.append(copy)
        return copy

    def sent(copy):
        copy.wait_send()
        pending[:] = [other for other in pending if other is not copy]

    xd, yd, zd = range(1, NX), range(1, NY), range(1, NZ)
    barrier = pltpu.get_barrier_semaphore()
    others = [dict(dk=1)] + [dict(dx=d) for d in xd] + [dict(dy=d) for d in yd] + [dict(dz=d) for d in zd]
    for where in others:
        pl.semaphore_signal(barrier, inc=1, device_id=peer(**where), device_id_type=MESH)

    weight_copy = pltpu.make_async_copy(weight_in, w_in, sems_l.at[0])
    weight_copy.start()

    rank_at = lax.broadcasted_iota(I32, (128, RANK), 0) * RANK + lax.broadcasted_iota(I32, (128, RANK), 1)
    base = rank_at * 747796405 + (seed[0] * 277803737 + 1013904223)

    @pl.loop(0, TC // 128)
    def _(part):
        mixed = base + (c * TC + part * 128) * (RANK * 747796405 % 2**32 - 2**32 * (RANK * 747796405 % 2**32 >= 2**31))
        mixed = jnp.bitwise_xor(mixed, jnp.right_shift(mixed, 15))
        mixed = mixed * 1664525
        mixed = jnp.bitwise_xor(mixed, jnp.right_shift(mixed, 13))
        value = jnp.bitwise_and(mixed, 65535).astype(F32) * (1.0 / 32768.0) - 1.0
        high, low = split(value)
        here = pl.ds(pl.multiple_of(part * 128, 128), 128)
        vh[here, :] = high
        vl[here, :] = low
        high, low = split(mom[:, here])
        mh[:, here] = high
        ml[:, here] = low

    mine = pl.ds(pl.multiple_of(k * HALF, HALF), HALF)
    other = pl.ds(pl.multiple_of((1 - k) * HALF, HALF), HALF)
    pp[...] = dot3((mh[other, :], ml[other, :]), (vh[...], vl[...]))
    pl.semaphore_wait(barrier, len(others))

    half_copy = send(pp, ch, dk=1)
    ph[...] = dot3((mh[mine, :], ml[mine, :]), (vh[...], vl[...]))
    half_copy.wait_recv()
    ph[...] += ch[...]
    copies = [send(ph.at[pl.ds(pl.multiple_of(lax.rem(z + d, NZ) * PZ, PZ), PZ)], zr.at[d - 1], dz=d) for d in zd]
    for copy in copies:
        copy.wait_recv()
    total = ph[pl.ds(pl.multiple_of(z * PZ, PZ), PZ), :]
    for d in zd:
        total = total + zr[d - 1]

    def p_rows(core, dz):
        return pl.ds(pl.multiple_of(core * HALF + lax.rem(z + dz, NZ) * PZ, PZ), PZ)

    pf[p_rows(k, 0), :] = total
    copies = [send(pf.at[p_rows(k, 0)], pf.at[p_rows(k, 0)], dz=d) for d in zd]
    siblings = [send(pf.at[p_rows(k, 0)], pf.at[p_rows(k, 0)], dk=1)]
    for d in zd:
        copies[d - 1].wait_recv()
        siblings.append(send(pf.at[p_rows(k, NZ - d)], pf.at[p_rows(k, NZ - d)], dk=1))
    for copy in siblings:
        copy.wait_recv()

    pt[...] = pf[...].T
    spot = k * 64 + z * 8
    for i in range(NX):
        gp[i * 8 : (i + 1) * 8, :] = pt[pl.ds(pl.multiple_of(i * XS + spot, 8), 8), :]
    gp2 = exact(gp[...], pf[...])
    gx[0] = gp2
    gcopies = [send(gx.at[0, pl.ds(pl.multiple_of(lax.rem(x + d, NX) * 8, 8), 8)], gx.at[d, pl.ds(0, 8)], dx=d) for d in xd]

    for i in range(NX):
        here = pl.ds(pl.multiple_of(i * XS, XS), XS)
        wp[here, :] = dot3(split(pt[here, :]), (mh[...], ml[...]))

    order = (1, 7, 2, 6, 3, 5, 4, 0)

    def a_rows(dx, dy):
        return pl.ds(pl.multiple_of(lax.rem(x + dx, NX) * XS + lax.rem(y + dy, NY) * SL, SL), SL)

    def b_block(dy):
        return pl.ds(pl.multiple_of(lax.rem(y + dy, NY) * YS, YS), YS)

    def b_rows(dx):
        return pl.ds(pl.multiple_of(y * YS + lax.rem(x + dx, NX) * SL, SL), SL)

    xcopies, ycopies, agy, agx, ring, bxc, bgx, bgather = {}, {}, {}, [], {}, {}, {}, {}

    halves = (pl.ds(0, HW), pl.ds(HW, HW))

    def wide_start(h):
        for e in order:
            for d in xd:
                xcopies[h, e, d] = send(wp.at[a_rows(d, e), halves[h]], xr.at[h, d - 1, e], dx=d)

    def wide_first(h, *es):
        for e in es:
            for d in xd:
                xcopies[h, e, d].wait_recv()
            rows = a_rows(0, e)
            total = wp[rows, halves[h]]
            for d in xd:
                total = total + xr[h, d - 1, e]
            wp[rows, halves[h]] = total
            if e:
                ycopies[h, e] = send(wp.at[rows, halves[h]], yr.at[h, e - 1], dy=e)

    def wide_second(h):
        for e in yd:
            ycopies[h, e].wait_recv()
        rows = a_rows(0, 0)
        total = wp[rows, halves[h]]
        for e in yd:
            total = total + yr[h, e - 1]
        wt[rows, halves[h]] = total
        for d in xd:
            agx.append(send(wt.at[rows, halves[h]], wt.at[rows, halves[h]], dx=d))
        for e in (1, 7, 2, 6, 3, 5, 4):
            agy[h, e] = send(wt.at[rows, halves[h]], wt.at[rows, halves[h]], dy=e)

    def wide_third(h, *es):
        for e in es:
            agy[h, e].wait_recv()
            rows = a_rows(0, NY - e)
            for d in xd:
                agx.append(send(wt.at[rows, halves[h]], wt.at[rows, halves[h]], dx=d))

    chunks = [(i, pl.ds(WIDE + begin, count), pl.ds(begin, count), reach) for i, (begin, count, reach) in enumerate(CHUNKS)]
    ways = ((1, 1), (NY - 1, -1))

    def block_at(way, d):
        return b_block(d if way[1] > 0 else NY - d)

    def narrow_send(i, cols, slot, w, d):
        ring[i, w, d] = send(wp.at[block_at(ways[w], d), cols], by.at[w, d - 1, :, slot], dy=ways[w][0])

    def narrow_start():
        for i, cols, slot, reach in chunks:
            for w in range(2):
                narrow_send(i, cols, slot, w, reach[w])

    def narrow_step(level):
        for i, cols, slot, reach in chunks:
            for w in range(2):
                d = reach[w] - level
                if d >= 1:
                    ring[i, w, d + 1].wait_recv()
                    wp[block_at(ways[w], d), cols] += by[w, d, :, slot]
                    narrow_send(i, cols, slot, w, d)

    def narrow_first():
        for i, cols, slot, reach in chunks:
            for w in range(2):
                ring[i, w, 1].wait_recv()
            wp[b_block(0), cols] += by[0, 0, :, slot] + by[1, 0, :, slot]
            for d in xd:
                bxc[i, d] = send(wp.at[b_rows(d), cols], bx.at[d - 1, :, slot], dx=d)

    def narrow_second():
        for i, cols, slot, reach in chunks:
            rows = b_rows(0)
            total = wp[rows, cols]
            for d in xd:
                bxc[i, d].wait_recv()
                total = total + bx[d - 1, :, slot]
            wt[rows, cols] = total
            for d in xd:
                bgx[i, d] = send(wt.at[rows, cols], wt.at[rows, cols], dx=d)

    def narrow_gather(level):
        for i, cols, slot, reach in chunks:
            if level == 0:
                for d in xd:
                    bgx[i, d].wait_recv()
            for w in range(2):
                if level < reach[w]:
                    if level:
                        bgather[i, w, level - 1].wait_recv()
                    rows = b_block(level if w else NY - level) if level else b_block(0)
                    bgather[i, w, level] = send(wt.at[rows, cols], wt.at[rows, cols], dy=ways[w][0])

    for copy in gcopies:
        copy.wait_recv()
    total = gx[0, pl.ds(pl.multiple_of(x * 8, 8), 8), :]
    for d in xd:
        total = total + gx[d, 0:8, :]
    g1[...] = total
    gcopies = [send(g1, gy.at[d - 1], dy=d) for d in yd]
    wide_start(0)
    narrow_start()
    wide_first(0, 1, 7)
    narrow_step(1)
    wide_first(0, 2)
    for copy in gcopies:
        copy.wait_recv()
    total = g1[...]
    for d in yd:
        total = total + gy[d - 1]
    own = pl.ds(pl.multiple_of(x * 8, 8), 8)
    gs[own, :] = total
    gcopies = [send(gs.at[own], gs.at[own], dx=d) for d in xd]
    wide_start(1)
    wide_first(0, 6, 3, 5, 4)
    for copy in gcopies:
        copy.wait_recv()

    def g_rows(i, core, dz):
        return pl.ds(pl.multiple_of(i * XS + core * 64 + lax.rem(z + dz, NZ) * 8, 8), 8)

    for i in range(NX):
        gram[g_rows(i, k, 0), :] = gs[i * 8 : (i + 1) * 8, :]
    zcopies = {}
    for i in range(NX):
        right = pl.ds(i * XS, RANK - i * XS)
        for d in zd:
            zcopies[i, d] = send(gram.at[g_rows(i, k, 0), right], gram.at[g_rows(i, k, 0), right], dz=d)
    narrow_step(2)
    wide_first(0, 0)
    wide_first(1, 1, 7)
    wide_second(0)
    narrow_step(3)
    wide_first(1, 2, 6)
    wide_third(0, 1, 7)
    scopies = []
    for i in range(NX):
        right = pl.ds(i * XS, RANK - i * XS)
        for d in zd:
            zcopies[i, d].wait_recv()
        rows = pl.ds(pl.multiple_of(i * XS + k * 64, 64), 64)
        scopies.append(send(gram.at[rows, right], gram.at[rows, right], dk=1))
    scopies[0].wait_recv()

    jobs = [
        [lambda: narrow_first(), lambda: wide_first(1, 3, 5), lambda: wide_third(0, 2, 6)],
        [lambda: wide_first(1, 4)],
        [lambda: narrow_second(), lambda: wide_third(0, 3, 5), lambda: wide_first(1, 0)],
        [lambda: wide_third(0, 4)],
        [lambda: narrow_gather(0), lambda: wide_second(1)],
        [],
        [lambda: wide_third(1, 1, 7)],
        [lambda: narrow_gather(1), lambda: wide_third(1, 2, 6)],
        [],
        [lambda: wide_third(1, 3, 5)],
        [lambda: narrow_gather(2), lambda: wide_third(1, 4)],
        [],
        [],
        [lambda: narrow_gather(3)],
        [],
        [],
    ]

    for b in range(NX):
        low, high = b * XS, (b + 1) * XS
        tiles = [gram[low + 8 * i : low + 8 * i + 8, low:high] for i in range(16)]
        for part in range(4):
            eliminate(tiles, range(4 * part, 4 * part + 4))
            for job in jobs[4 * b + part]:
                job()
        block = jnp.concatenate(tiles, axis=0)
        if b == 0:
            for copy in scopies[1:]:
                copy.wait_recv()
            for copy in list(zcopies.values()) + scopies:
                sent(copy)
        panel = exact(block, gram[low:high, :])
        gram[low:high, :] = panel
        gram[low:high, low:high] = block
        if b < NX - 1:
            factor = gram[low:high, high:].T
            cross = exact(factor, gram[low:high, :])
            old = gram[high:, :]
            spot_lane = lax.broadcasted_iota(I32, (RANK - high, RANK), 1)
            gram[high:, :] = jnp.where((spot_lane >= low) & (spot_lane < high), 0.0, old) - cross

    inverse = gram
    q_in = split(pf[...])
    for b in range(NX):
        high = (b + 1) * XS
        qb[:, b * XS : high] = dot3((q_in[0][:, :high], q_in[1][:, :high]), split(inverse[b * XS : high, :high]), NT)

    for copy in agx + [bgather[i, w, reach[w] - 1] for i, _, _, reach in chunks for w in range(2)]:
        copy.wait_recv()
    factors = [split(inverse[b * XS : (b + 1) * XS, : (b + 1) * XS]) for b in range(NX)]
    squares = [jnp.zeros((XS, 128), F32) for _ in range(NX)]
    for begin, count in PARTS:
        here = slice(begin, begin + count)
        high, low = split(wt[:, here])
        for b in range(NX):
            end = (b + 1) * XS
            rows = slice(b * XS, end)
            piece = dot3(factors[b], (high[:end], low[:end]))
            rt[rows, here] = piece
            for i in range(count // 128):
                squares[b] += piece[:, i * 128 : (i + 1) * 128] ** 2

    sub = lax.broadcasted_iota(I32, (8, 128), 0)
    packed = jnp.zeros((8, 128), F32)
    for b in range(NX):
        packed = jnp.where(sub == b, exact(jnp.ones((8, 128), F32), squares[b], NT), packed)
    sq[...] = packed
    copies = [send(sq, sqr.at[d - 1], dz=d) for d in zd]

    basis = qb[...].astype(BF16)
    for begin, count in PARTS:
        here = slice(begin, begin + count)
        high, low = split(rt[:, here])
        rh[:, here] = high
        rl[:, here] = low
        mom_new[:, here] = mom[:, here] - (1.0 - MOMENTUM_DECAY) * dot(basis, high)
    mom_copy = pltpu.make_async_copy(mom_new, mom_out, sems_l.at[1])
    mom_copy.start()
    for copy in copies:
        copy.wait_recv()
    for d in zd:
        packed = packed + sqr[d - 1]
    sqc[0] = packed
    send(sqc.at[0], sqc.at[1], dk=1).wait_recv()
    scales = lax.rsqrt((sqc[0] + sqc[1]) * (1.0 / COLS) + EPSILON)

    scale_row = jnp.concatenate([scales[b : b + 1, :] for b in range(NX)], axis=1)
    weight_copy.wait()
    scaled = split(qb[...] * (scale_row * (ROWS / RANK) ** 0.5))
    for begin, count in PARTS:
        here = slice(begin, begin + count)
        update = dot3(scaled, (rh[:, here], rl[:, here]))
        w_new[:, here] = (w_in[:, here].astype(F32) - rate[0] * update).astype(BF16)
    weight_out_copy = pltpu.make_async_copy(w_new, weight_out, sems_l.at[2])
    weight_out_copy.start()
    picked = lax.broadcasted_iota(I32, (SL, RANK), 1) == r * SL + lax.broadcasted_iota(I32, (SL, RANK), 0)
    own_scale = jnp.sum(jnp.where(picked, scale_row, 0.0), axis=1, keepdims=True)
    next_new[...] = rt[pl.ds(pl.multiple_of(r * SL, SL), SL), :] * own_scale
    next_copy = pltpu.make_async_copy(next_new, next_out, sems_l.at[3])
    next_copy.start()
    mom_copy.wait()
    weight_out_copy.wait()
    next_copy.wait()
    for copy in pending:
        copy.wait_send()


SENDS = 1 + 7 + 7 + 8 + 3 + 7 + 48 + 3 + 28 + 4 + 14 + 14 + 48 + 3 * (7 + 3 + 3 + 7) + 7 + 1


def per_device(momentum, weight, init_seed, step_rate):
    vmem, smem, anywhere = (pl.BlockSpec(memory_space=space) for space in (pltpu.VMEM, pltpu.SMEM, pl.ANY))
    return pl.pallas_call(
        update_tile,
        out_shape=[
            jax.ShapeDtypeStruct((TR, TC), F32),
            jax.ShapeDtypeStruct((TR, TC), BF16),
            jax.ShapeDtypeStruct((SL, TC), F32),
        ],
        in_specs=[vmem, anywhere, smem, smem],
        out_specs=[anywhere, anywhere, anywhere],
        scratch_shapes=[
            pltpu.VMEM((TR, TC), BF16),
            pltpu.VMEM((TR, TC), F32),
            pltpu.VMEM((TR, TC), BF16),
            pltpu.VMEM((SL, TC), F32),
            pltpu.VMEM((TR, RANK), F32),
            pltpu.VMEM((RANK, TC), F32),
            pltpu.VMEM((RANK, TC), BF16),
            pltpu.VMEM((RANK, TC), BF16),
            pltpu.VMEM((TR, TC), BF16),
            pltpu.VMEM((TR, TC), BF16),
            pltpu.VMEM((TC, RANK), BF16),
            pltpu.VMEM((TC, RANK), BF16),
            pltpu.VMEM((HALF, RANK), F32),
            pltpu.VMEM((HALF, RANK), F32),
            pltpu.VMEM((HALF, RANK), F32),
            pltpu.VMEM((NZ - 1, PZ, RANK), F32),
            pltpu.VMEM((TR, RANK), F32),
            pltpu.VMEM((RANK, TR), F32),
            pltpu.VMEM((32, TR), F32),
            pltpu.VMEM((NX, 32, RANK), F32),
            pltpu.VMEM((8, RANK), F32),
            pltpu.VMEM((NY - 1, 8, RANK), F32),
            pltpu.VMEM((32, RANK), F32),
            pltpu.VMEM((RANK, RANK), F32),
            pltpu.VMEM((RANK, TC), F32),
            pltpu.VMEM((2, NX - 1, NY, SL, HW), F32),
            pltpu.VMEM((2, NY - 1, SL, HW), F32),
            pltpu.VMEM((NX - 1, SL, NARROW), F32),
            pltpu.VMEM((2, 4, YS, NARROW), F32),
            pltpu.VMEM((RANK, TC), F32),
            pltpu.VMEM((8, 128), F32),
            pltpu.VMEM((NZ - 1, 8, 128), F32),
            pltpu.VMEM((2, 8, 128), F32),
            pltpu.SemaphoreType.DMA((SENDS,)),
            pltpu.SemaphoreType.DMA((SENDS,)),
            pltpu.SemaphoreType.DMA((4,)),
        ],
        compiler_params=pltpu.CompilerParams(collective_id=0, has_side_effects=True, vmem_limit_bytes=56 * 2**20),
        name="update_tile",
    )(momentum, weight, init_seed, step_rate)


def solution(mesh):
    placed = (P("row", "col"), P("row", "col"), P(), P())
    return jax.shard_map(
        per_device,
        mesh=mesh,
        in_specs=placed,
        out_specs=(P("row", "col"), P("row", "col"), P("row", "col")),
        check_vma=False,
    )
```
